32 devices in a mesh: ep: 4 (over y, core), dp: 8 (over z, x).
Axes of the slice: x: 2, y: 2, z: 4, core: 2. Of those that a mesh axis runs over, the one named last changes fastest.
Arguments:
- fwd_tokens: bfloat16 [512, 2048], P(('ep', 'dp')), may hold values from -6 to 6
- fwd_routes: int32 [512, 2], P(('ep', 'dp')), may hold values from 0 to 3, as said below
- fwd_weights: float32 [512, 2], P(('ep', 'dp')), may hold values from 0.05 to 0.4
- bwd_grads: bfloat16 [512, 2048], P(('ep', 'dp')), may hold values from -6 to 6
- bwd_routes: int32 [512, 2], P(('ep', 'dp')), may hold values from 0 to 3, as said below
- bwd_weights: float32 [512, 2], P(('ep', 'dp')), may hold values from 0.05 to 0.4
- bwd_saved: bfloat16 [4, 256, 2048], P('ep', 'dp'), may hold values from -6 to 6
- w_gate: bfloat16 [4, 2048, 384], P('ep'), may hold values from -0.125 to 0.125
- w_up: bfloat16 [4, 2048, 384], P('ep'), may hold values from -0.125 to 0.125
- w_down: bfloat16 [4, 384, 2048], P('ep'), may hold values from -0.3125 to 0.3125
Outputs:
- fwd_out: bfloat16 [512, 2048], P(('ep', 'dp'))
- bwd_input_grad: bfloat16 [512, 2048], P(('ep', 'dp'))
- down_grad: float32 [4, 2048, 384], P('ep', 'dp')
The draws below stay inside these ranges and needn't reach their ends.
Inputs may be any that keep to these rules, and one draw needn't show every extreme that they name: `fwd_routes`: each token names 2 different experts, and the 16 tokens of each aligned block (one device's tokens) name every expert exactly 8 times. `bwd_routes`: each token names 2 different experts, and the 16 tokens of each aligned block (one device's tokens) name every expert exactly 8 times.
All inputs are finite; a program needn't handle non-finite values.
Results may differ from the reference program's by a relative error of at most 0.0064.
Values may be sent and summed in bfloat16 or wider, within the bound.
A program may use at most 64 MiB of HBM per device.

```python
import math
import jax
import jax.numpy as jnp
from jax import lax

D = 2048
FF = 384
TOK = 16
EXPERTS = 4
TOP = 2
TOKENS = 512
ROWS = 256
N_EP = 4
N_DP = 8


def route_group(key):
    first, second, third = jax.random.split(key, 3)
    expert_perm = jax.random.permutation(first, EXPERTS)
    offsets = jax.random.permutation(second, EXPERTS)[:TOP]
    shuffle = jax.random.permutation(third, EXPERTS)
    position = (shuffle[:, None] + offsets[None, :]) % EXPERTS
    return expert_perm[position]


def route_block(key):
    keys_all = jax.random.split(key, TOK // EXPERTS + 1)
    grouped = jax.vmap(route_group)(keys_all[1:]).reshape(TOK, TOP)
    reorder = jax.random.permutation(keys_all[0], TOK)
    return grouped[reorder]


def route_table(key):
    keys_all = jax.random.split(key, TOKENS // TOK)
    return jax.vmap(route_block)(keys_all).reshape(TOKENS, TOP).astype(jnp.int32)


def draw_fwd_routes(key, part):
    return route_table(jax.random.fold_in(key, 11))


def draw_bwd_routes(key, part):
    return route_table(jax.random.fold_in(key, 23))


def raised(array, rng, source, target, shards_of, factor):
    def block_of(dim):
        return (jnp.arange(array.shape[dim]) // (array.shape[dim] // shards_of)).reshape((-1,) + (1,) * (array.ndim - 1 - dim))

    one_side = jax.random.permutation(rng, shards_of)[block_of(target)]
    far = (block_of(target) + shards_of // 2) % shards_of
    return jnp.where((block_of(source) == one_side) | (block_of(source) == far), factor * array, array)


def level_of(key, shape, cuts, smallest, top_value):
    gain, own = 1.0, jax.random.fold_in(key, 6)
    for dim, parts in cuts:
        steps = jnp.exp(jax.random.uniform(jax.random.fold_in(own, dim), (parts,), jnp.float32, smallest / len(cuts), top_value / len(cuts)))
        gain = gain * jnp.repeat(steps, shape[dim] // parts).reshape([-1 if axis == dim else 1 for axis in range(len(shape))])
    return gain


def bell_draw(key, shape, deviation, limit, pieces=(), kind=jnp.bfloat16):
    level = level_of(key, shape, pieces, -0.22, 0.18) if pieces else 1.0
    drawn = jax.random.normal(key, shape, jnp.float32) * deviation * level
    return jnp.minimum(jnp.maximum(drawn, -limit), limit).astype(kind)


def gaussian_with(stream_key, dims, spread, bound, shards, heavy, kind=jnp.bfloat16):
    entries = spread * jax.random.normal(stream_key, dims, jnp.float32)
    if shards:
        entries = entries * level_of(stream_key, dims, shards, -0.22, 0.18)
    return jnp.clip(raised(entries, jax.random.fold_in(stream_key, 3), *heavy), -bound, bound).astype(kind)


def setup_inputs(seed: int = 0) -> dict:
    key_of = jax.random.split(jax.random.key(seed), 11)
    fwd_tokens = bell_draw(key_of[0], (TOKENS, D), 1.0, 6.0, ((0, 32),))
    fwd_routes = draw_fwd_routes(jax.random.fold_in(key_of[10], 71), 0)
    fwd_weights = jnp.clip(jnp.exp(math.log(0.4) - 2.0794415 * jax.random.uniform(key_of[2], (TOKENS, TOP), jnp.float32) ** level_of(key_of[2], (TOKENS, TOP), ((0, 32),), -0.2, 0.2)), 0.05, 0.4)
    bwd_grads = gaussian_with(key_of[3], (TOKENS, D), 1.0, 6.0, ((0, 32),), (0, 1, 32, 2.75))
    bwd_routes = draw_bwd_routes(jax.random.fold_in(key_of[10], 71), 0)
    bwd_weights = jnp.clip(jnp.exp(math.log(0.4) - 2.0794415 * jax.random.uniform(key_of[5], (TOKENS, TOP), jnp.float32) ** level_of(key_of[5], (TOKENS, TOP), ((0, 32),), -0.2, 0.2)), 0.05, 0.4)
    bwd_saved = bell_draw(key_of[6], (EXPERTS, ROWS, D), 1.0, 6.0, ((0, 4), (1, 8)))
    w_gate = bell_draw(key_of[7], (EXPERTS, D, FF), D ** -0.5, 0.125, ((0, 4),))
    w_up = bell_draw(key_of[8], (EXPERTS, D, FF), D ** -0.5, 0.125, ((0, 4),))
    w_down = bell_draw(key_of[9], (EXPERTS, FF, D), FF ** -0.5, 0.3125, ((0, 4),))
    return {"fwd_tokens": fwd_tokens, "fwd_routes": fwd_routes, "fwd_weights": fwd_weights, "bwd_grads": bwd_grads, "bwd_routes": bwd_routes, "bwd_weights": bwd_weights, "bwd_saved": bwd_saved, "w_gate": w_gate, "w_up": w_up, "w_down": w_down}


def slot_order(routes):
    blocks = routes.shape[0] // TOK
    block_of = jnp.arange(routes.shape[0], dtype=jnp.int32) // TOK
    source = (block_of % N_DP) * N_EP + block_of // N_DP
    sort_keys = routes * blocks + source[:, None]
    ranked = jnp.argsort(sort_keys.reshape(-1), stable=True).astype(jnp.int32)
    return ranked.reshape(EXPERTS, -1)


def reference(fwd_tokens, fwd_routes, fwd_weights, bwd_grads, bwd_routes, bwd_weights, bwd_saved, w_gate, w_up, w_down):
    fwd_slots = slot_order(fwd_routes)
    fwd_flat = fwd_weights.reshape(-1)
    bwd_slots = slot_order(bwd_routes)
    bwd_flat = bwd_weights.reshape(-1)
    contract_last = (((1,), (1,)), ((), ()))
    contract_rows = (((0,), (0,)), ((), ()))

    def forward_step(summed, inputs):
        picked, gate_w, up_w, down_w = inputs
        token_ids = picked // TOP
        expert_in = fwd_tokens[token_ids]
        gate_pre = jnp.dot(expert_in, gate_w, preferred_element_type=jnp.float32)
        up_pre = jnp.dot(expert_in, up_w, preferred_element_type=jnp.float32)
        hidden = (jax.nn.silu(gate_pre) * up_pre).astype(jnp.bfloat16)
        expert_out = jnp.dot(hidden, down_w, preferred_element_type=jnp.float32).astype(jnp.bfloat16)
        summed = summed.at[token_ids].add(fwd_flat[picked][:, None] * expert_out.astype(jnp.float32))
        return summed, None

    fwd_sum, unused = lax.scan(forward_step, jnp.zeros(fwd_tokens.shape, jnp.float32), (fwd_slots, w_gate, w_up, w_down))

    def backward_step(summed, inputs):
        picked, saved_rows, gate_w, up_w, down_w = inputs
        token_ids = picked // TOP
        cot_rows = (bwd_flat[picked][:, None] * bwd_grads[token_ids].astype(jnp.float32)).astype(jnp.bfloat16)
        gate_pre = jnp.dot(saved_rows, gate_w, preferred_element_type=jnp.float32)
        up_pre = jnp.dot(saved_rows, up_w, preferred_element_type=jnp.float32)
        sigma = jax.nn.sigmoid(gate_pre)
        hidden = (gate_pre * sigma * up_pre).astype(jnp.bfloat16)
        dact = lax.dot_general(cot_rows, down_w, contract_last, preferred_element_type=jnp.float32)
        dgate = (dact * up_pre * sigma * (1.0 + gate_pre * (1.0 - sigma))).astype(jnp.bfloat16)
        dup_rows = (dact * gate_pre * sigma).astype(jnp.bfloat16)
        row_grad = lax.dot_general(dgate, gate_w, contract_last, preferred_element_type=jnp.float32)
        row_grad = (row_grad + lax.dot_general(dup_rows, up_w, contract_last, preferred_element_type=jnp.float32)).astype(jnp.bfloat16)
        summed = summed.at[token_ids].add(row_grad.astype(jnp.float32))
        weight_term = lax.dot_general(cot_rows, hidden, contract_rows, preferred_element_type=jnp.float32)
        return summed, weight_term

    bwd_sum, down_grad = lax.scan(backward_step, jnp.zeros(bwd_grads.shape, jnp.float32), (bwd_slots, bwd_saved, w_gate, w_up, w_down))
    return fwd_sum.astype(jnp.bfloat16), bwd_sum.astype(jnp.bfloat16), down_grad
```

```python
import functools

import jax
import jax.numpy as jnp
from jax import lax
from jax.experimental import pallas as pl
from jax.experimental.pallas import tpu as pltpu
from jax.sharding import PartitionSpec as P

BF16, F32 = jnp.bfloat16, jnp.float32
LAST = (((1,), (1,)), ((), ()))
FIRST = (((0,), (0,)), ((), ()))


def matmul(a, b, dims=(((1,), (0,)), ((), ()))):
    return lax.dot_general(a, b, dims, preferred_element_type=F32)


def kernel(
    experts, groups, slots,
    tok_hbm, routes_a_hbm, mix_a_hbm, grad_hbm, routes_b_hbm, mix_b_hbm, saved_hbm, gate_hbm, up_hbm, down_hbm,
    out_a, out_b, out_w,
    tok, routes_a, mix_a, grad, routes_b, mix_b, saved, wgu, wd,
    send_a, send_b, got_a, got_b, ret_a, ret_b, home_a, home_b,
    cols, cols_all, act_all,
    load_sem, ep_send, ep_recv, dp_send, dp_recv,
):
    ep, dp = lax.axis_index("ep"), lax.axis_index("dp")
    width, ff = tok.shape[1], wd.shape[0]
    half = width // 2
    rows = experts * slots

    loads = []
    for src, dst in (
        (routes_b_hbm, routes_b), (mix_b_hbm, mix_b), (grad_hbm, grad),
        (routes_a_hbm, routes_a), (mix_a_hbm, mix_a), (tok_hbm, tok),
        (saved_hbm.at[0], saved),
        (gate_hbm.at[0], wgu.at[:, pl.ds(0, ff)]), (up_hbm.at[0], wgu.at[:, pl.ds(ff, ff)]),
        (down_hbm.at[0], wd),
    ):
        copy = pltpu.make_async_copy(src, dst, load_sem.at[len(loads)])
        copy.start()
        loads.append(copy)

    barrier = pltpu.get_barrier_semaphore()
    for k in range(1, experts):
        pl.semaphore_signal(barrier, inc=1, device_id={"ep": lax.rem(ep + k, experts)}, device_id_type=pl.DeviceIdType.MESH)
    for k in range(1, groups):
        pl.semaphore_signal(barrier, inc=1, device_id={"dp": lax.rem(dp + k, groups)}, device_id_type=pl.DeviceIdType.MESH)

    def exchange(which, src, dst):
        copies = []
        for k in range(1, experts):
            peer = lax.rem(ep + k, experts)
            copy = pltpu.make_async_remote_copy(
                src_ref=src.at[peer], dst_ref=dst.at[ep], send_sem=ep_send.at[which, k], recv_sem=ep_recv.at[which, k],
                device_id={"ep": peer}, device_id_type=pl.DeviceIdType.MESH,
            )
            copy.start()
            copies.append(copy)
        dst[ep] = src[ep]
        return copies

    def spread(which, src_of, dst):
        copies = []
        for k in range(1, groups):
            peer = lax.rem(dp + k, groups)
            copy = pltpu.make_async_remote_copy(
                src_ref=src_of(peer), dst_ref=dst.at[dp], send_sem=dp_send.at[which, k], recv_sem=dp_recv.at[which, k],
                device_id={"dp": peer}, device_id_type=pl.DeviceIdType.MESH,
            )
            copy.start()
            copies.append(copy)
        return copies

    def table(routes, mix):
        top, tokens = routes.shape
        shape = (2 * rows, tokens)
        index = lax.broadcasted_iota(jnp.int32, shape, 0)
        expert = index // (2 * slots)
        slot = (index % slots).astype(F32)
        hit = jnp.zeros(shape, F32)
        weight = jnp.zeros(shape, F32)
        for k in range(top):
            same = routes[pl.ds(k, 1), :] == expert
            hit = jnp.where(same, 1.0, hit)
            weight = weight + jnp.where(same, mix[pl.ds(k, 1), :], 0.0)
        square = (tokens, tokens)
        earlier = lax.broadcasted_iota(jnp.int32, square, 0) < lax.broadcasted_iota(jnp.int32, square, 1)
        before = matmul(hit.astype(BF16), jnp.where(earlier, 1.0, 0.0).astype(BF16))
        chosen = jnp.where(before == slot, hit, 0.0)
        part = (index // slots) % 2
        halves = [jnp.where(part == h, chosen, 0.0) for h in range(2)]
        return halves, chosen * weight, weight

    def pick(halves, source):
        return matmul(halves[0].astype(BF16), source[:, :half]) + matmul(halves[1].astype(BF16), source[:, half:])

    def of_half(x, h):
        return x.reshape(experts, 2, slots, x.shape[-1])[:, h].reshape(rows, x.shape[-1])

    def folded(x):
        x = x.reshape(experts, slots, width)
        return jnp.concatenate([x[:, :, :half], x[:, :, half:]], axis=1)

    def flat(ref):
        return ref[...].reshape(2 * rows, half)

    for copy in loads[:3]:
        copy.wait()
    halves_b, scaled_b, _ = table(routes_b, mix_b)
    scale = jnp.sum(scaled_b, axis=1, keepdims=True)
    send_b[...] = (pick(halves_b, grad) * scale).astype(BF16).reshape(send_b.shape)
    for copy in loads[3:6]:
        copy.wait()
    halves_a, _, weight_a = table(routes_a, mix_a)
    send_a[...] = pick(halves_a, tok).astype(BF16).reshape(send_a.shape)

    pl.semaphore_wait(barrier, experts + groups - 2)
    b_out = exchange(0, send_b, got_b)
    a_out = exchange(1, send_a, got_a)

    for copy in loads[6:9]:
        copy.wait()
    pre = matmul(saved[...], wgu[...])
    gate, up = pre[:, :ff], pre[:, ff:]
    sig = 1.0 / (1.0 + jnp.exp(-gate))
    swish = gate * sig
    act_all[dp] = (swish * up).astype(BF16)
    acts = spread(0, lambda peer: act_all.at[dp], act_all)
    slope = up * sig * (1.0 + gate * (1.0 - sig))
    loads[9].wait()

    for copy in b_out:
        copy.wait_recv()
    wide = flat(got_b).astype(F32)
    for g in range(groups):
        piece = width // groups
        h, at = g * piece // half, g * piece % half
        cols[g] = of_half(wide[:, at:at + piece], h).astype(BF16)
    col_out = spread(1, lambda peer: cols.at[peer], cols_all)
    cols_all[dp] = cols[dp]
    cot = flat(got_b)
    dact = of_half(matmul(cot, wd[:, :half], LAST), 0) + of_half(matmul(cot, wd[:, half:], LAST), 1)
    inner = jnp.concatenate([(dact * slope).astype(BF16), (dact * swish).astype(BF16)], axis=1)
    ret_b[...] = folded(matmul(inner, wgu[...], LAST)).astype(BF16)
    b_back = exchange(2, ret_b, home_b)

    for copy in a_out:
        copy.wait_recv()
    x = flat(got_a)
    pre = of_half(matmul(x, wgu[:half, :]), 0) + of_half(matmul(x, wgu[half:, :]), 1)
    gate, up = pre[:, :ff], pre[:, ff:]
    act = (gate / (1.0 + jnp.exp(-gate)) * up).astype(BF16)
    ret_a[...] = folded(matmul(act, wd[...])).astype(BF16)
    a_back = exchange(3, ret_a, home_a)

    for copy in acts:
        copy.wait_recv()
    for copy in col_out:
        copy.wait_recv()
    step = min(groups, max(1, 256 // rows))

    def term(i):
        left = cols_all[pl.ds(i * step, step)].reshape(step * rows, width // groups)
        return matmul(left, act_all[pl.ds(i * step, step)].reshape(step * rows, ff), FIRST)

    if step == groups:
        out_w[0] = term(0)
    else:
        out_w[0] = lax.fori_loop(1, groups // step, lambda i, total: total + term(i), term(0))

    for copy in b_back:
        copy.wait_recv()
    came = flat(home_b)
    for h in range(2):
        out_b[:, h * half:(h + 1) * half] = matmul(halves_b[h].astype(BF16), came, FIRST).astype(BF16)
    for copy in a_back:
        copy.wait_recv()
    came = flat(home_a)
    for h in range(2):
        mixing = halves_a[h] * weight_a
        high = mixing.astype(BF16)
        low = (mixing - high.astype(F32)).astype(BF16)
        out_a[:, h * half:(h + 1) * half] = (matmul(high, came, FIRST) + matmul(low, came, FIRST)).astype(BF16)

    for copy in (*b_out, *a_out, *acts, *col_out, *b_back, *a_back):
        copy.wait_send()


def on_device(tok, routes_a, mix_a, grad, routes_b, mix_b, saved, gate, up, down):
    experts, groups = lax.axis_size("ep"), lax.axis_size("dp")
    tokens, width = tok.shape
    top = routes_a.shape[1]
    ff = down.shape[1]
    slots = tokens * top // experts
    rows = experts * slots
    piece = width // groups
    block = pltpu.VMEM((experts, 2 * slots, width // 2), BF16)
    table = [pltpu.VMEM((top, tokens), jnp.int32), pltpu.VMEM((top, tokens), F32)]
    return pl.pallas_call(
        functools.partial(kernel, experts, groups, slots),
        out_shape=(
            jax.ShapeDtypeStruct((tokens, width), BF16),
            jax.ShapeDtypeStruct((tokens, width), BF16),
            jax.ShapeDtypeStruct((1, piece, ff), F32),
        ),
        in_specs=[pl.BlockSpec(memory_space=pltpu.MemorySpace.HBM)] * 10,
        out_specs=[pl.BlockSpec(memory_space=pltpu.VMEM)] * 3,
        scratch_shapes=[
            pltpu.VMEM((tokens, width), BF16), *table,
            pltpu.VMEM((tokens, width), BF16), *table,
            pltpu.VMEM((rows, width), BF16),
            pltpu.VMEM((width, 2 * ff), BF16),
            pltpu.VMEM((ff, width), BF16),
            *[block] * 8,
            pltpu.VMEM((groups, rows, piece), BF16),
            pltpu.VMEM((groups, rows, piece), BF16),
            pltpu.VMEM((groups, rows, ff), BF16),
            pltpu.SemaphoreType.DMA((10,)),
            pltpu.SemaphoreType.DMA((4, experts)),
            pltpu.SemaphoreType.DMA((4, experts)),
            pltpu.SemaphoreType.DMA((2, groups)),
            pltpu.SemaphoreType.DMA((2, groups)),
        ],
        compiler_params=pltpu.CompilerParams(collective_id=0, has_side_effects=True, vmem_limit_bytes=40 * 2**20),
    )(tok, routes_a.T, mix_a.T, grad, routes_b.T, mix_b.T, saved, gate, up, down)


def solution(mesh):
    by_token = P(("ep", "dp"), None)
    by_row = P("ep", "dp", None)
    by_expert = P("ep", None, None)
    return jax.shard_map(
        on_device,
        mesh=mesh,
        in_specs=(by_token,) * 6 + (by_row,) + (by_expert,) * 3,
        out_specs=(by_token, by_token, by_row),
        check_vma=False,
    )
```

```python
import functools

import jax
import jax.numpy as jnp
from jax import lax
from jax.experimental import pallas as pl
from jax.experimental.pallas import tpu as pltpu
from jax.sharding import PartitionSpec as P

BF16, F32 = jnp.bfloat16, jnp.float32
LAST = (((1,), (1,)), ((), ()))
FIRST = (((0,), (0,)), ((), ()))


def matmul(a, b, dims=(((1,), (0,)), ((), ()))):
    return lax.dot_general(a, b, dims, preferred_element_type=F32)


def kernel(
    experts, groups, slots,
    tok_hbm, routes_a_hbm, mix_a_hbm, grad_hbm, routes_b_hbm, mix_b_hbm, saved_hbm, gate_hbm, up_hbm, down_hbm,
    out_a, out_b, out_w,
    tok, routes_a, mix_a, grad, routes_b, mix_b, saved, wgu, wd,
    send_a, send_b, got_a, got_b, ret_a, ret_b, home_a, home_b,
    cols, cols_all, act_all,
    load_sem, ep_send, ep_recv, dp_send, dp_recv,
):
    ep, dp = lax.axis_index("ep"), lax.axis_index("dp")
    width, ff = tok.shape[1], wd.shape[0]
    half = width // 2
    rows = experts * slots

    loads = []
    for src, dst in (
        (routes_b_hbm, routes_b), (mix_b_hbm, mix_b), (grad_hbm, grad),
        (routes_a_hbm, routes_a), (mix_a_hbm, mix_a), (tok_hbm, tok),
        (saved_hbm.at[0], saved),
        (gate_hbm.at[0], wgu.at[:, pl.ds(0, ff)]), (up_hbm.at[0], wgu.at[:, pl.ds(ff, ff)]),
        (down_hbm.at[0], wd),
    ):
        copy = pltpu.make_async_copy(src, dst, load_sem.at[len(loads)])
        copy.start()
        loads.append(copy)

    barrier = pltpu.get_barrier_semaphore()
    for k in range(1, experts):
        pl.semaphore_signal(barrier, inc=1, device_id={"ep": lax.rem(ep + k, experts)}, device_id_type=pl.DeviceIdType.MESH)
    for k in range(1, groups):
        pl.semaphore_signal(barrier, inc=1, device_id={"dp": lax.rem(dp + k, groups)}, device_id_type=pl.DeviceIdType.MESH)

    def exchange(which, src, dst):
        copies = []
        for k in range(1, experts):
            peer = lax.rem(ep + k, experts)
            copy = pltpu.make_async_remote_copy(
                src_ref=src.at[peer], dst_ref=dst.at[ep], send_sem=ep_send.at[which, k], recv_sem=ep_recv.at[which, k],
                device_id={"ep": peer}, device_id_type=pl.DeviceIdType.MESH,
            )
            copy.start()
            copies.append(copy)
        dst[ep] = src[ep]
        return copies

    def spread(which, src_of, dst):
        copies = []
        for k in range(1, groups):
            peer = lax.rem(dp + k, groups)
            copy = pltpu.make_async_remote_copy(
                src_ref=src_of(peer), dst_ref=dst.at[dp], send_sem=dp_send.at[which, k], recv_sem=dp_recv.at[which, k],
                device_id={"dp": peer}, device_id_type=pl.DeviceIdType.MESH,
            )
            copy.start()
            copies.append(copy)
        return copies

    def table(routes, mix):
        top, tokens = routes.shape
        shape = (2 * rows, tokens)
        index = lax.broadcasted_iota(jnp.int32, shape, 0)
        expert = index // (2 * slots)
        slot = (index % slots).astype(F32)
        hit = jnp.zeros(shape, F32)
        weight = jnp.zeros(shape, F32)
        for k in range(top):
            same = routes[pl.ds(k, 1), :] == expert
            hit = jnp.where(same, 1.0, hit)
            weight = weight + jnp.where(same, mix[pl.ds(k, 1), :], 0.0)
        square = (tokens, tokens)
        earlier = lax.broadcasted_iota(jnp.int32, square, 0) < lax.broadcasted_iota(jnp.int32, square, 1)
        before = matmul(hit.astype(BF16), jnp.where(earlier, 1.0, 0.0).astype(BF16))
        chosen = jnp.where(before == slot, hit, 0.0)
        part = (index // slots) % 2
        halves = [jnp.where(part == h, chosen, 0.0) for h in range(2)]
        return halves, chosen * weight, weight

    def pick(halves, source):
        return matmul(halves[0].astype(BF16), source[:, :half]) + matmul(halves[1].astype(BF16), source[:, half:])

    def of_half(x, h):
        return x.reshape(experts, 2, slots, x.shape[-1])[:, h].reshape(rows, x.shape[-1])

    def folded(x):
        x = x.reshape(experts, slots, width)
        return jnp.concatenate([x[:, :, :half], x[:, :, half:]], axis=1)

    def flat(ref):
        return ref[...].reshape(2 * rows, half)

    for copy in loads[:3]:
        copy.wait()
    halves_b, scaled_b, _ = table(routes_b, mix_b)
    scale = jnp.sum(scaled_b, axis=1, keepdims=True)
    send_b[...] = (pick(halves_b, grad) * scale).astype(BF16).reshape(send_b.shape)
    for copy in loads[3:6]:
        copy.wait()
    halves_a, _, weight_a = table(routes_a, mix_a)
    send_a[...] = pick(halves_a, tok).astype(BF16).reshape(send_a.shape)

    pl.semaphore_wait(barrier, experts + groups - 2)
    b_out = exchange(0, send_b, got_b)
    a_out = exchange(1, send_a, got_a)

    for copy in loads[6:9]:
        copy.wait()
    pre = matmul(saved[...], wgu[...])
    gate, up = pre[:, :ff], pre[:, ff:]
    sig = 1.0 / (1.0 + jnp.exp(-gate))
    swish = gate * sig
    act_all[dp] = (swish * up).astype(BF16)
    acts = spread(0, lambda peer: act_all.at[dp], act_all)
    slope = up * sig * (1.0 + gate * (1.0 - sig))
    loads[9].wait()

    for copy in b_out:
        copy.wait_recv()
    wide = flat(got_b).astype(F32)
    for g in range(groups):
        piece = width // groups
        h, at = g * piece // half, g * piece % half
        cols[g] = of_half(wide[:, at:at + piece], h).astype(BF16)
    col_out = spread(1, lambda peer: cols.at[peer], cols_all)
    cols_all[dp] = cols[dp]
    cot = flat(got_b)
    dact = of_half(matmul(cot, wd[:, :half], LAST), 0) + of_half(matmul(cot, wd[:, half:], LAST), 1)
    inner = jnp.concatenate([(dact * slope).astype(BF16), (dact * swish).astype(BF16)], axis=1)
    ret_b[...] = folded(matmul(inner, wgu[...], LAST)).astype(BF16)
    b_back = exchange(2, ret_b, home_b)

    for copy in a_out:
        copy.wait_recv()
    x = flat(got_a)
    pre = of_half(matmul(x, wgu[:half, :]), 0) + of_half(matmul(x, wgu[half:, :]), 1)
    gate, up = pre[:, :ff], pre[:, ff:]
    act = (gate / (1.0 + jnp.exp(-gate)) * up).astype(BF16)
    ret_a[...] = folded(matmul(act, wd[...])).astype(BF16)
    a_back = exchange(3, ret_a, home_a)

    for copy in acts:
        copy.wait_recv()
    for copy in col_out:
        copy.wait_recv()
    step = min(groups, max(1, 256 // rows))

    def term(i):
        left = cols_all[pl.ds(i * step, step)].reshape(step * rows, width // groups)
        return matmul(left, act_all[pl.ds(i * step, step)].reshape(step * rows, ff), FIRST)

    if step == groups:
        out_w[0] = term(0)
    else:
        out_w[0] = lax.fori_loop(1, groups // step, lambda i, total: total + term(i), term(0))

    for copy in b_back:
        copy.wait_recv()
    came = flat(home_b)
    for h in range(2):
        out_b[:, h * half:(h + 1) * half] = matmul(halves_b[h].astype(BF16), came, FIRST).astype(BF16)
    for copy in a_back:
        copy.wait_recv()
    came = flat(home_a)
    for h in range(2):
        mixing = halves_a[h] * weight_a
        high = mixing.astype(BF16)
        low = (mixing - high.astype(F32)).astype(BF16)
        out_a[:, h * half:(h + 1) * half] = (matmul(high, came, FIRST) + matmul(low, came, FIRST)).astype(BF16)

    for copy in (*b_out, *a_out, *acts, *col_out, *b_back, *a_back):
        copy.wait_send()


def store(*refs):
    sems = refs[6]
    copies = [pltpu.make_async_copy(refs[i], refs[3 + i], sems.at[i]) for i in range(3)]
    for copy in copies:
        copy.start()
    for copy in copies:
        copy.wait()


def on_device(tok, routes_a, mix_a, grad, routes_b, mix_b, saved, gate, up, down):
    experts, groups = lax.axis_size("ep"), lax.axis_size("dp")
    tokens, width = tok.shape
    top = routes_a.shape[1]
    ff = down.shape[1]
    slots = tokens * top // experts
    rows = experts * slots
    piece = width // groups
    block = pltpu.VMEM((experts, 2 * slots, width // 2), BF16)
    table = [pltpu.VMEM((top, tokens), jnp.int32), pltpu.VMEM((top, tokens), F32)]
    outs = pl.pallas_call(
        functools.partial(kernel, experts, groups, slots),
        out_shape=(
            jax.ShapeDtypeStruct((tokens, width), BF16),
            jax.ShapeDtypeStruct((tokens, width), BF16),
            jax.ShapeDtypeStruct((1, piece, ff), F32),
        ),
        in_specs=[pl.BlockSpec(memory_space=pltpu.MemorySpace.HBM)] * 10,
        out_specs=[pl.BlockSpec(memory_space=pltpu.VMEM)] * 3,
        scratch_shapes=[
            pltpu.VMEM((tokens, width), BF16), *table,
            pltpu.VMEM((tokens, width), BF16), *table,
            pltpu.VMEM((rows, width), BF16),
            pltpu.VMEM((width, 2 * ff), BF16),
            pltpu.VMEM((ff, width), BF16),
            *[block] * 8,
            pltpu.VMEM((groups, rows, piece), BF16),
            pltpu.VMEM((groups, rows, piece), BF16),
            pltpu.VMEM((groups, rows, ff), BF16),
            pltpu.SemaphoreType.DMA((10,)),
            pltpu.SemaphoreType.DMA((4, experts)),
            pltpu.SemaphoreType.DMA((4, experts)),
            pltpu.SemaphoreType.DMA((2, groups)),
            pltpu.SemaphoreType.DMA((2, groups)),
        ],
        compiler_params=pltpu.CompilerParams(collective_id=0, has_side_effects=True, vmem_limit_bytes=40 * 2**20),
    )(*[
        pltpu.with_memory_space_constraint(x, pltpu.MemorySpace.HBM)
        for x in (tok, routes_a.T, mix_a.T, grad, routes_b.T, mix_b.T, saved, gate, up, down)
    ])
    return pl.pallas_call(
        store,
        out_shape=tuple(jax.ShapeDtypeStruct(x.shape, x.dtype) for x in outs),
        in_specs=[pl.BlockSpec(memory_space=pl.ANY)] * 3,
        out_specs=[pl.BlockSpec(memory_space=pl.ANY)] * 3,
        scratch_shapes=[pltpu.SemaphoreType.DMA((3,))],
        compiler_params=pltpu.CompilerParams(vmem_limit_bytes=2**20),
    )(*outs)


def solution(mesh):
    by_token = P(("ep", "dp"), None)
    by_row = P("ep", "dp", None)
    by_expert = P("ep", None, None)
    return jax.shard_map(
        on_device,
        mesh=mesh,
        in_specs=(by_token,) * 6 + (by_row,) + (by_expert,) * 3,
        out_specs=(by_token, by_token, by_row),
        check_vma=False,
    )
```

```python
import functools

import jax
import jax.numpy as jnp
from jax import lax
from jax.experimental import pallas as pl
from jax.experimental.pallas import tpu as pltpu
from jax.sharding import PartitionSpec as P

BF16, F32 = jnp.bfloat16, jnp.float32
LAST = (((1,), (1,)), ((), ()))
FIRST = (((0,), (0,)), ((), ()))


def matmul(a, b, dims=(((1,), (0,)), ((), ()))):
    return lax.dot_general(a, b, dims, preferred_element_type=F32)


def kernel(
    experts, groups, slots,
    tok_hbm, routes_a_hbm, mix_a_hbm, grad_hbm, routes_b_hbm, mix_b_hbm, saved_hbm, gate_hbm, up_hbm, down_hbm,
    out_a, out_b, out_w,
    tok, routes_a, mix_a, grad, routes_b, mix_b, saved, wgu, wd,
    send_a, send_b, got_a, got_b, ret_a, ret_b, home_a, home_b,
    cols, cols_all, act_all,
    load_sem, ep_send, ep_recv, dp_send, dp_recv,
):
    ep, dp = lax.axis_index("ep"), lax.axis_index("dp")
    width, ff = tok.shape[1], wd.shape[0]
    half = width // 2
    rows = experts * slots

    loads = []
    for src, dst in (
        (routes_b_hbm, routes_b), (mix_b_hbm, mix_b), (grad_hbm, grad),
        (routes_a_hbm, routes_a), (mix_a_hbm, mix_a), (tok_hbm, tok),
        (saved_hbm.at[0], saved),
        *(
            (src.at[0, pl.ds(h * half, half)], wgu.at[pl.ds(h * half, half), pl.ds(at, ff)])
            for h in range(2) for src, at in ((gate_hbm, 0), (up_hbm, ff))
        ),
        (down_hbm.at[0], wd),
    ):
        copy = pltpu.make_async_copy(src, dst, load_sem.at[len(loads)])
        copy.start()
        loads.append(copy)

    barrier = pltpu.get_barrier_semaphore()
    for k in range(1, experts):
        pl.semaphore_signal(barrier, inc=1, device_id={"ep": lax.rem(ep + k, experts)}, device_id_type=pl.DeviceIdType.MESH)
    for k in range(1, groups):
        pl.semaphore_signal(barrier, inc=1, device_id={"dp": lax.rem(dp + k, groups)}, device_id_type=pl.DeviceIdType.MESH)

    def exchange(which, src, dst):
        copies = []
        for k in range(1, experts):
            peer = lax.rem(ep + k, experts)
            copy = pltpu.make_async_remote_copy(
                src_ref=src.at[peer], dst_ref=dst.at[ep], send_sem=ep_send.at[which, k], recv_sem=ep_recv.at[which, k],
                device_id={"ep": peer}, device_id_type=pl.DeviceIdType.MESH,
            )
            copy.start()
            copies.append(copy)
        dst[ep] = src[ep]
        return copies

    def spread(which, src_of, dst):
        copies = []
        for k in range(1, groups):
            peer = lax.rem(dp + k, groups)
            copy = pltpu.make_async_remote_copy(
                src_ref=src_of(peer), dst_ref=dst.at[dp], send_sem=dp_send.at[which, k], recv_sem=dp_recv.at[which, k],
                device_id={"dp": peer}, device_id_type=pl.DeviceIdType.MESH,
            )
            copy.start()
            copies.append(copy)
        return copies

    def table(routes, mix):
        top, tokens = routes.shape
        shape = (2 * rows, tokens)
        index = lax.broadcasted_iota(jnp.int32, shape, 0)
        expert = index // (2 * slots)
        slot = (index % slots).astype(F32)
        hit = jnp.zeros(shape, F32)
        weight = jnp.zeros(shape, F32)
        for k in range(top):
            same = routes[pl.ds(k, 1), :] == expert
            hit = jnp.where(same, 1.0, hit)
            weight = weight + jnp.where(same, mix[pl.ds(k, 1), :], 0.0)
        square = (tokens, tokens)
        earlier = lax.broadcasted_iota(jnp.int32, square, 0) < lax.broadcasted_iota(jnp.int32, square, 1)
        before = matmul(hit.astype(BF16), jnp.where(earlier, 1.0, 0.0).astype(BF16))
        chosen = jnp.where(before == slot, hit, 0.0)
        part = (index // slots) % 2
        halves = [jnp.where(part == h, chosen, 0.0) for h in range(2)]
        return halves, chosen * weight, weight

    def pick(halves, source):
        return matmul(halves[0].astype(BF16), source[:, :half]) + matmul(halves[1].astype(BF16), source[:, half:])

    def of_half(x, h):
        return x.reshape(experts, 2, slots, x.shape[-1])[:, h].reshape(rows, x.shape[-1])

    def folded(x):
        x = x.reshape(experts, slots, width)
        return jnp.concatenate([x[:, :, :half], x[:, :, half:]], axis=1)

    def flat(ref):
        return ref[...].reshape(2 * rows, half)

    for copy in loads[:6]:
        copy.wait()
    halves_b, scaled_b, _ = table(routes_b, mix_b)
    scale = jnp.sum(scaled_b, axis=1, keepdims=True)
    send_b[...] = (pick(halves_b, grad) * scale).astype(BF16).reshape(send_b.shape)
    halves_a, _, weight_a = table(routes_a, mix_a)
    send_a[...] = pick(halves_a, tok).astype(BF16).reshape(send_a.shape)

    pl.semaphore_wait(barrier, experts + groups - 2)
    b_out = exchange(0, send_b, got_b)
    a_out = exchange(1, send_a, got_a)

    for copy in loads[6:9]:
        copy.wait()
    pre = matmul(saved[:, :half], wgu[:half, :])
    for copy in loads[9:11]:
        copy.wait()
    pre = pre + matmul(saved[:, half:], wgu[half:, :])
    gate, up = pre[:, :ff], pre[:, ff:]
    sig = 1.0 / (1.0 + jnp.exp(-gate))
    swish = gate * sig
    act_all[dp] = (swish * up).astype(BF16)
    acts = spread(0, lambda peer: act_all.at[dp], act_all)
    slope = up * sig * (1.0 + gate * (1.0 - sig))
    loads[11].wait()

    for copy in b_out:
        copy.wait_recv()
    wide = flat(got_b).astype(F32)
    for g in range(groups):
        piece = width // groups
        h, at = g * piece // half, g * piece % half
        cols[g] = of_half(wide[:, at:at + piece], h).astype(BF16)
    col_out = spread(1, lambda peer: cols.at[peer], cols_all)
    cols_all[dp] = cols[dp]
    cot = flat(got_b)
    dact = of_half(matmul(cot, wd[:, :half], LAST), 0) + of_half(matmul(cot, wd[:, half:], LAST), 1)
    both = jnp.concatenate([(dact * slope).astype(BF16), (dact * swish).astype(BF16)], axis=1)
    ret_b[...] = folded(matmul(both, wgu[...], LAST)).astype(BF16)
    b_back = exchange(2, ret_b, home_b)

    for copy in a_out:
        copy.wait_recv()
    x = flat(got_a)
    pre = of_half(matmul(x, wgu[:half, :]), 0) + of_half(matmul(x, wgu[half:, :]), 1)
    gate, up = pre[:, :ff], pre[:, ff:]
    act = (gate / (1.0 + jnp.exp(-gate)) * up).astype(BF16)
    ret_a[...] = folded(matmul(act, wd[...])).astype(BF16)
    a_back = exchange(3, ret_a, home_a)

    for copy in acts:
        copy.wait_recv()
    for copy in col_out:
        copy.wait_recv()
    step = min(groups, max(1, 256 // rows))

    def term(i):
        left = cols_all[pl.ds(i * step, step)].reshape(step * rows, width // groups)
        return matmul(left, act_all[pl.ds(i * step, step)].reshape(step * rows, ff), FIRST)

    if step == groups:
        out_w[0] = term(0)
    else:
        out_w[0] = lax.fori_loop(1, groups // step, lambda i, total: total + term(i), term(0))

    for copy in b_back:
        copy.wait_recv()
    came = flat(home_b)
    for h in range(2):
        out_b[:, h * half:(h + 1) * half] = matmul(halves_b[h].astype(BF16), came, FIRST).astype(BF16)
    for copy in a_back:
        copy.wait_recv()
    came = flat(home_a)
    for h in range(2):
        mixing = halves_a[h] * weight_a
        high = mixing.astype(BF16)
        low = (mixing - high.astype(F32)).astype(BF16)
        out_a[:, h * half:(h + 1) * half] = (matmul(high, came, FIRST) + matmul(low, came, FIRST)).astype(BF16)

    for copy in (*b_out, *a_out, *acts, *col_out, *b_back, *a_back):
        copy.wait_send()


def store(*refs):
    sems = refs[6]
    copies = [pltpu.make_async_copy(refs[i], refs[3 + i], sems.at[i]) for i in range(3)]
    for copy in copies:
        copy.start()
    for copy in copies:
        copy.wait()


def on_device(tok, routes_a, mix_a, grad, routes_b, mix_b, saved, gate, up, down):
    experts, groups = lax.axis_size("ep"), lax.axis_size("dp")
    tokens, width = tok.shape
    top = routes_a.shape[1]
    ff = down.shape[1]
    slots = tokens * top // experts
    rows = experts * slots
    piece = width // groups
    block = pltpu.VMEM((experts, 2 * slots, width // 2), BF16)
    table = [pltpu.VMEM((top, tokens), jnp.int32), pltpu.VMEM((top, tokens), F32)]
    outs = pl.pallas_call(
        functools.partial(kernel, experts, groups, slots),
        out_shape=(
            jax.ShapeDtypeStruct((tokens, width), BF16),
            jax.ShapeDtypeStruct((tokens, width), BF16),
            jax.ShapeDtypeStruct((1, piece, ff), F32),
        ),
        in_specs=[pl.BlockSpec(memory_space=pltpu.MemorySpace.HBM)] * 10,
        out_specs=[pl.BlockSpec(memory_space=pltpu.VMEM)] * 3,
        scratch_shapes=[
            pltpu.VMEM((tokens, width), BF16), *table,
            pltpu.VMEM((tokens, width), BF16), *table,
            pltpu.VMEM((rows, width), BF16),
            pltpu.VMEM((width, 2 * ff), BF16),
            pltpu.VMEM((ff, width), BF16),
            *[block] * 8,
            pltpu.VMEM((groups, rows, piece), BF16),
            pltpu.VMEM((groups, rows, piece), BF16),
            pltpu.VMEM((groups, rows, ff), BF16),
            pltpu.SemaphoreType.DMA((12,)),
            pltpu.SemaphoreType.DMA((4, experts)),
            pltpu.SemaphoreType.DMA((4, experts)),
            pltpu.SemaphoreType.DMA((2, groups)),
            pltpu.SemaphoreType.DMA((2, groups)),
        ],
        compiler_params=pltpu.CompilerParams(collective_id=0, has_side_effects=True, vmem_limit_bytes=40 * 2**20),
    )(*[
        pltpu.with_memory_space_constraint(x, pltpu.MemorySpace.HBM)
        for x in (tok, routes_a.T, mix_a.T, grad, routes_b.T, mix_b.T, saved, gate, up, down)
    ])
    return pl.pallas_call(
        store,
        out_shape=tuple(jax.ShapeDtypeStruct(x.shape, x.dtype) for x in outs),
        in_specs=[pl.BlockSpec(memory_space=pl.ANY)] * 3,
        out_specs=[pl.BlockSpec(memory_space=pl.ANY)] * 3,
        scratch_shapes=[pltpu.SemaphoreType.DMA((3,))],
        compiler_params=pltpu.CompilerParams(vmem_limit_bytes=2**20),
    )(*outs)


def solution(mesh):
    by_token = P(("ep", "dp"), None)
    by_row = P("ep", "dp", None)
    by_expert = P("ep", None, None)
    return jax.shard_map(
        on_device,
        mesh=mesh,
        in_specs=(by_token,) * 6 + (by_row,) + (by_expert,) * 3,
        out_specs=(by_token, by_token, by_row),
        check_vma=False,
    )
```
